32 devices in a mesh: grp: 2 (over x), fac: 16 (over z, y, core).
Axes of the slice: x: 2, y: 2, z: 4, core: 2. Of those that a mesh axis runs over, the one named last changes fastest.
Arguments:
- model_blocks: bfloat16 [1024, 16384], P(('grp', 'fac')), parts along dimension 0, may hold values from -0.01171875 to 0.01171875
- task_owner: int32 [4096, 1], P(('grp', 'fac')), parts along dimension 0, may hold values from 0 to 15; in each aligned block of 128 rows (0 to 127, 128 to 255, ...) at most 16 rows name the same one
- task_block: int32 [4096], P(('grp', 'fac')), parts along dimension 0, may hold values from 0 to 31
- baseline_of_task: int32 [4096], P(('grp', 'fac')), parts along dimension 0, may hold values from 0 to 63
- coords: float32 [4096, 3, 384], P(('grp', 'fac')), parts along dimension 0, may hold values from -2 to 2
- vis_count: int32 [4096], P(('grp', 'fac')), parts along dimension 0, may hold values from 1 to 384, as said below
Outputs:
- model_visibilities: float32 [128, 2, 384], P(('grp', 'fac')), parts along dimension 0
The draws below stay inside these ranges and needn't reach their ends.
There are 2 independent parts, one for each index of `grp`. The reference program is written for one: setup_inputs(seed, part) draws one part's arguments, and reference() takes and returns one part's arrays. A program takes and returns all parts, laid end to end along the dimension named above; each array names one. Nothing has to cross between parts.
Inputs may be any that keep to these rules, and one draw needn't show every extreme that they name: `task_owner`: within the tasks of one device no facet owner is named by more than 16 tasks. `vis_count`: some task has all 384 visibilities live.
All inputs are finite; a program needn't handle non-finite values.
Results may differ from the reference program's by a relative error of at most 0.0033.
Values may be sent and summed in bfloat16 or wider, within the bound.
A program may use at most 64 MiB of HBM per device.

```python
import math
import jax
import jax.numpy as jnp
import numpy as np
from jax import lax

SUB = 64
LAYERS = 2
VIS = 384
BLK_DEV = 32
TASK_DEV = 128
FACETS = 16
CAP = 16
FLAT = 16384
BLOCKS = 512
TASK_TOTAL = 2048
BASELINE_TOTAL = 64


def draw_coords(key, part):
    key = jax.random.fold_in(key, 5)
    first = jax.random.fold_in(key, 0)
    shape = (TASK_TOTAL, 3, VIS)
    values = jax.random.uniform(first, shape, jnp.float32, -2.0, 2.0)
    return values


def draw_vis_count(key, part):
    key = jax.random.fold_in(key, 11)
    counts = jax.random.randint(key, (TASK_TOTAL,), 1, VIS + 1, dtype=jnp.int32)
    return counts.at[0].set(VIS)


def with_ends(values, stream_key, low, top_value):
    shape = values.shape
    place = [jax.random.randint(jax.random.fold_in(stream_key, axis), (), 0, shape[axis]) for axis in range(len(shape))]
    values = values.at[tuple(place)].set(low)
    longest = shape.index(max(shape))
    place[longest] = (place[longest] + 1) % shape[longest]
    return values.at[tuple(place)].set(top_value)


def block_levels(own_key, shape, shards, low, top_value):
    factor_of, own = 1.0, jax.random.fold_in(own_key, 6)
    for dim, parts in shards:
        heights = jnp.exp(jax.random.uniform(jax.random.fold_in(own, dim), (parts,), jnp.float32, low / len(shards), top_value / len(shards)))
        factor_of = factor_of * jnp.repeat(heights, shape[dim] // parts).reshape([-1 if axis == dim else 1 for axis in range(len(shape))])
    return factor_of


def routed_block(rng, own, number, rows, number_of, top, limit, slope):
    order = jax.random.permutation(rng, number_of)
    heavy_load, usual = shares(number_of, rows * top, limit, slope, True), shares(number_of, rows * top, limit, slope, False)
    places = jnp.arange(number_of)

    def named(tallies, turn):
        used = int((tallies > 0).sum())
        fixed = max(1, used // 4)
        moved = fixed + (places - fixed + turn * (used - fixed)) % max(1, number_of - fixed)
        return jnp.zeros((number_of,), jnp.int32).at[order[jnp.where(places < fixed, places, moved)]].set(jnp.asarray(tallies, jnp.int32))

    tallies = jnp.where(number % 4 == 0, named(heavy_load, number // 4), named(usual, number - number // 4 - 1))
    mixed = jax.random.permutation(jax.random.fold_in(own, 3), number_of)
    donor, receiver = mixed[0:number_of // 2 * 2:2], mixed[1:number_of // 2 * 2:2]
    slack = jnp.minimum(tallies[donor] - 1, limit - tallies[receiver]) // 2
    slack = jnp.where((donor == order[0]) | (receiver == order[0]) | (tallies[receiver] == 0), 0, jnp.maximum(slack, 0))
    moved = jax.random.randint(jax.random.fold_in(own, 4), (number_of // 2,), 0, 1 << 20) % (slack + 1)
    tallies = tallies.at[donor].add(-moved).at[receiver].add(moved)
    labels = jnp.searchsorted(jnp.cumsum(tallies), jnp.arange(rows * top), side="right").astype(jnp.int32)
    table = labels.reshape(top, rows).T
    table = table[jax.random.permutation(jax.random.fold_in(own, 1), rows)]
    turn = jax.random.randint(jax.random.fold_in(own, 2), (rows, 1), 0, top)
    return jnp.take_along_axis(table, (jnp.arange(top)[None, :] + turn) % top, axis=1)


def shares(number_of, total, limit, slope, full):
    portions = [(1 << 20) // math.isqrt(grade ** slope) + 1 for grade in range(1, number_of + 1)]
    largest = limit if full else min(limit, max(-(-total // number_of), total * portions[0] // sum(portions)))
    least = 1 if total - largest >= number_of - 1 else 0
    holding, rest = [largest] + [least] * (number_of - 1), total - largest - least * (number_of - 1)
    while rest > 0:
        free = [i for i in range(1, number_of) if holding[i] < largest] or [i for i in range(1, number_of) if holding[i] < limit]
        pool, budget = sum([portions[i] for i in free]), rest
        for i in free:
            extra = min(limit - holding[i], max(1, budget * portions[i] // pool), rest)
            holding[i] = holding[i] + extra
            rest = rest - extra
    return np.array(holding)


def centred(own_key, extent, width, most, cuts=(), held_as=jnp.bfloat16):
    entries = width * jax.random.normal(own_key, extent, jnp.float32)
    if cuts:
        entries = entries * block_levels(own_key, extent, cuts, -0.22, 0.18)
    return jnp.clip(entries, -most, most).astype(held_as)


def setup_inputs(seed: int = 0, part: int = 0) -> dict:
    streams_of = jax.random.split(jax.random.key(seed), 7)
    part_keys = jax.random.split(jax.random.fold_in(streams_of[6], part), 7)
    model_blocks = centred(part_keys[0], (BLOCKS, FLAT), (1.0 / (8 * SUB)), 0.01171875, ((0, 16),))
    task_owner_keys = jax.random.split(jax.random.fold_in(part_keys[1], 1), TASK_TOTAL // TASK_DEV)
    task_owner_turns = jax.random.permutation(jax.random.fold_in(part_keys[1], 3), TASK_TOTAL // TASK_DEV)
    task_owner = jax.vmap(lambda own, number: routed_block(jax.random.fold_in(part_keys[1], 2), own, number, TASK_DEV, FACETS, 1, CAP, 2))(task_owner_keys, task_owner_turns).reshape((TASK_TOTAL, 1))
    task_block = with_ends(jax.random.randint(part_keys[2], (TASK_TOTAL,), 0, BLK_DEV), jax.random.fold_in(part_keys[2], 1), 0, BLK_DEV - 1).astype(jnp.int32)
    baseline_of_task = with_ends(jax.random.randint(part_keys[3], (TASK_TOTAL,), 0, BASELINE_TOTAL), jax.random.fold_in(part_keys[3], 1), 0, BASELINE_TOTAL - 1).astype(jnp.int32)
    coords = draw_coords(jax.random.fold_in(jax.random.fold_in(streams_of[6], part), 71), part)
    vis_count = draw_vis_count(jax.random.fold_in(jax.random.fold_in(streams_of[6], part), 71), part)
    return dict(model_blocks=model_blocks, task_owner=task_owner, task_block=task_block, baseline_of_task=baseline_of_task, coords=coords, vis_count=vis_count)


def contributions(block_rows, task_coords, live_count):
    group = block_rows.shape[0]
    samples = task_coords.shape[2]
    offsets = jnp.arange(SUB, dtype=jnp.float32) - SUB / 2
    column_arg = ((-0.5 * math.pi) * task_coords[:, 1][:, None, :]) * offsets[None, :, None]
    column_basis = jnp.concatenate([jnp.cos(column_arg), jnp.sin(column_arg)], axis=2).astype(jnp.bfloat16)
    row_arg = (-0.5 * math.pi) * offsets[None, :, None] * task_coords[:, 0][:, None, :]
    row_real_part = lax.optimization_barrier(jnp.cos(row_arg).astype(jnp.bfloat16)).astype(jnp.float32)
    row_im = lax.optimization_barrier(jnp.sin(row_arg).astype(jnp.bfloat16)).astype(jnp.float32)
    pixels = block_rows.reshape(group, LAYERS * 2 * SUB, SUB)
    product = jnp.einsum('grm,gmj->grj', pixels.astype(jnp.float32), column_basis.astype(jnp.float32))
    product = product.reshape(group, LAYERS, 2, SUB, 2 * samples)
    real_rows = product[:, :, 0]
    imag_rows = product[:, :, 1]
    inner_re = real_rows[..., :samples] - imag_rows[..., samples:]
    inner_im = real_rows[..., samples:] + imag_rows[..., :samples]
    row_real_part = row_real_part[:, None]
    row_im = row_im[:, None]
    layer_re = jnp.sum(row_real_part * inner_re - row_im * inner_im, axis=2)
    layer_im = jnp.sum(row_real_part * inner_im + row_im * inner_re, axis=2)
    layer_offsets = 2.0 * jnp.arange(LAYERS, dtype=jnp.float32) - (LAYERS - 1)
    w_phase = -math.pi * task_coords[:, 2][:, None, :] * layer_offsets[None, :, None]
    cosine = jnp.cos(w_phase)
    sines = jnp.sin(w_phase)
    total_re = jnp.sum(cosine * layer_re - sines * layer_im, axis=1)
    total_im = jnp.sum(cosine * layer_im + sines * layer_re, axis=1)
    live_mask = jnp.arange(samples, dtype=jnp.int32)[None, :] < live_count[:, None]
    stacked = jnp.stack([total_re, total_im], axis=1)
    return jnp.where(live_mask[:, None, :], stacked, jnp.zeros_like(stacked))


def reference(model_blocks, task_owner, task_block, baseline_of_task, coords, vis_count):
    global_ids = (task_owner[:, 0] * BLK_DEV + task_block).astype(jnp.int32)

    def one_group(inputs):
        ids_here, coords_here, count_here = inputs
        return contributions(model_blocks[ids_here], coords_here, count_here)

    result = lax.map(one_group, (global_ids.reshape(TASK_TOTAL // 8, 8), coords.reshape(TASK_TOTAL // 8, 8, 3, VIS), vis_count.reshape(TASK_TOTAL // 8, 8)))
    block_contribution = result.reshape(TASK_TOTAL, 2, VIS)
    return jax.ops.segment_sum(block_contribution, baseline_of_task, num_segments=BASELINE_TOTAL)
```

```python
import functools
import math

import jax
import jax.numpy as jnp
import numpy as np
from jax import lax
from jax.experimental import pallas as pl
from jax.experimental.pallas import tpu as pltpu
from jax.sharding import PartitionSpec as P

SUB = 64
HALF = SUB // 2
LAYERS = 2
BL_DEV = 4
GROUP = 16
META = 128


def fold_blocks(model_blocks):
    blocks = model_blocks.shape[0]
    pixels = model_blocks.reshape(blocks * LAYERS * 2 * SUB, SUB)
    fold = np.zeros((SUB, SUB), np.float32)
    for n in range(HALF):
        fold[HALF + n, n] = fold[HALF - 1 - n, n] = 1.0
        fold[HALF + n, HALF + n], fold[HALF - 1 - n, HALF + n] = 1.0, -1.0
    fold = jnp.asarray(fold, jnp.bfloat16)
    x = jnp.dot(pixels, fold, preferred_element_type=jnp.float32)
    x = x.reshape(blocks, LAYERS, 2, SUB, SUB)
    plus, minus = x[:, 0] + x[:, 1], x[:, 0] - x[:, 1]
    x = jnp.stack([plus, minus], axis=1)
    upper, lower = x[:, :, :, HALF:], x[:, :, :, HALF - 1 :: -1]
    even, odd = upper + lower, upper - lower

    def parts(rows, turn):
        out_re, out_im = [], []
        for k in range(2):
            for m in range(2):
                re = rows[:, k, 0, :, m * HALF : (m + 1) * HALF]
                im = rows[:, k, 1, :, m * HALF : (m + 1) * HALF]
                times = (k - m + turn) % 4
                for _ in range(times):
                    re, im = -im, re
                out_re.append(re)
                out_im.append(im)
        return jnp.concatenate(out_re, axis=2), jnp.concatenate(out_im, axis=2)

    even_re, even_im = parts(even, 0)
    odd_re, odd_im = parts(odd, 3)
    return jnp.concatenate([even_re, even_im, odd_re, odd_im], axis=1).astype(jnp.bfloat16)


def sincos(x):
    n = jnp.floor(x + 0.5)
    t = (x - n) * (0.5 * math.pi)
    t2 = t * t
    s = t * (1.0 + t2 * (-1.0 / 6 + t2 * (1.0 / 120 + t2 * (-1.0 / 5040 + t2 * (1.0 / 362880)))))
    c = 1.0 + t2 * (-0.5 + t2 * (1.0 / 24 + t2 * (-1.0 / 720 + t2 * (1.0 / 40320 - t2 * (1.0 / 3628800)))))
    turn = n.astype(jnp.int32)
    swap = (turn & 1) == 1
    sine = jnp.where(swap, c, s)
    cosine = jnp.where(swap, s, c)
    sine = jnp.where((turn & 2) == 2, -sine, sine)
    cosine = jnp.where(((turn + 1) & 2) == 2, -cosine, cosine)
    return sine, cosine


def powers(x, cos_ref, sin_ref):
    s0, c0 = sincos(0.5 * x)
    s1, c1 = 2.0 * s0 * c0, 1.0 - 2.0 * s0 * s0
    s, c = s0, c0
    lanes = x.shape[1] // 128
    for p in range(HALF):
        for a in range(lanes):
            cos_ref[a, pl.ds(p, GROUP, stride=HALF), :] = c[:, a * 128 : (a + 1) * 128]
            sin_ref[a, pl.ds(p, GROUP, stride=HALF), :] = s[:, a * 128 : (a + 1) * 128]
        if p < HALF - 1:
            s, c = s * c1 + c * s1, c * c1 - s * s1
    return s0, c0


def load(ref, t):
    lanes = ref.shape[0]
    return jnp.concatenate([ref[a, pl.ds(t * HALF, HALF), :] for a in range(lanes)], axis=1)


def compute_kernel(block_ids, baselines, slots_ref, folded_ref, out_ref, ru, su, rv, sv, cw_ref, sw_ref, sums):
    g = pl.program_id(0)
    vis = out_ref.shape[1] // 2

    @pl.when(g == 0)
    def _():
        out_ref[...] = jnp.zeros_like(out_ref)

    u, v, w = (slots_ref[:, i * vis : (i + 1) * vis] for i in range(3))
    us, uc = powers(u, ru, su)
    vs, vc = powers(v, rv, sv)
    ws, wc = sincos(2.0 * w)
    cw_ref[...] = wc
    sw_ref[...] = ws
    for t in range(GROUP):
        c, s = load(rv, t), load(sv, t)
        cw, sw = cw_ref[t : t + 1, :], sw_ref[t : t + 1, :]
        basis = jnp.concatenate([c * cw, s * cw, c * sw, s * sw], axis=0).astype(jnp.bfloat16)
        inner = jnp.dot(folded_ref[block_ids[g * GROUP + t]], basis, preferred_element_type=jnp.float32)
        rc, rs = load(ru, t), load(su, t)
        re = jnp.sum(rc * inner[:HALF] + rs * inner[2 * HALF : 3 * HALF], axis=0, keepdims=True)
        im = jnp.sum(rc * inner[HALF : 2 * HALF] + rs * inner[3 * HALF :], axis=0, keepdims=True)
        sums[t : t + 1, :vis] = re
        sums[t : t + 1, vis:] = im
    hc, hs = uc * vc - us * vs, uc * vs + us * vc
    re, im = sums[:, :vis], sums[:, vis:]
    live = lax.broadcasted_iota(jnp.int32, (GROUP, vis), 1).astype(jnp.float32) < slots_ref[:, 3 * vis : 3 * vis + 1]
    sums[:, :vis] = jnp.where(live, re * hc - im * hs, 0.0)
    sums[:, vis:] = jnp.where(live, re * hs + im * hc, 0.0)
    for t in range(GROUP):
        b = baselines[g * GROUP + t]
        out_ref[pl.ds(b, 1), :] += sums[t : t + 1, :]


def compute(slots, block_ids, baselines, folded, n_baselines, vis):
    n, width = slots.shape
    lanes = vis // 128
    table = pltpu.VMEM((lanes, GROUP * HALF, 128), jnp.float32)
    return pl.pallas_call(
        compute_kernel,
        out_shape=jax.ShapeDtypeStruct((n_baselines, 2 * vis), jnp.float32),
        grid_spec=pltpu.PrefetchScalarGridSpec(
            num_scalar_prefetch=2,
            grid=(n // GROUP,),
            in_specs=[
                pl.BlockSpec((GROUP, width), lambda g, *_: (g, 0)),
                pl.BlockSpec(folded.shape, lambda g, *_: (0, 0, 0)),
            ],
            out_specs=pl.BlockSpec((n_baselines, 2 * vis), lambda g, *_: (0, 0)),
            scratch_shapes=[
                table,
                table,
                table,
                table,
                pltpu.VMEM((GROUP, vis), jnp.float32),
                pltpu.VMEM((GROUP, vis), jnp.float32),
                pltpu.VMEM((GROUP, 2 * vis), jnp.float32),
            ],
        ),
        compiler_params=pltpu.CompilerParams(vmem_limit_bytes=32 * 1024 * 1024),
        cost_estimate=pl.CostEstimate(flops=n * 128 * 128 * 768, bytes_accessed=4 * n * width, transcendentals=0),
    )(block_ids, baselines, slots, folded)


def body(model_blocks, task_owner, task_block, baseline_of_task, coords, vis_count):
    facets = lax.axis_size("fac")
    tasks, _, vis = coords.shape
    capacity = max(2, 2 * tasks // facets)
    slots = facets * capacity
    owner = task_owner[:, 0]
    same = owner[:, None] == owner[None, :]
    before = jnp.arange(tasks)[None, :] < jnp.arange(tasks)[:, None]
    rank = jnp.sum((same & before).astype(jnp.int32), axis=1)
    slot = owner * capacity + rank
    hit = jnp.arange(slots, dtype=jnp.int32)[:, None] == slot[None, :]
    source = jnp.sum(jnp.where(hit, jnp.arange(tasks, dtype=jnp.int32)[None, :], 0), axis=1)
    meta = jnp.stack([vis_count, task_block, baseline_of_task], axis=1)
    meta = jnp.sum(jnp.where(hit[:, :, None], meta[None], 0), axis=1).astype(jnp.float32)
    meta = jnp.pad(meta, ((0, 0), (0, META - 3)))
    rows = coords.reshape(tasks, 3 * vis)[source]
    sent = jnp.concatenate([rows, meta], axis=1)
    sent = sent.reshape(facets, capacity, 3 * vis + META)
    got = lax.all_to_all(sent, "fac", split_axis=0, concat_axis=0, tiled=True).reshape(slots, 3 * vis + META)
    folded = fold_blocks(model_blocks)
    block_ids = got[:, 3 * vis + 1].astype(jnp.int32)
    baselines = got[:, 3 * vis + 2].astype(jnp.int32)
    partial = compute(got, block_ids, baselines, folded, BL_DEV * facets, vis)
    shares = partial.reshape(facets, BL_DEV, 2 * vis)
    shares = lax.all_to_all(shares, "fac", split_axis=0, concat_axis=0, tiled=True)
    return jnp.sum(shares, axis=0).reshape(BL_DEV, 2, vis)


def solution(mesh):
    placed = (
        P(("grp", "fac"), None),
        P(("grp", "fac"), None),
        P(("grp", "fac")),
        P(("grp", "fac")),
        P(("grp", "fac"), None, None),
        P(("grp", "fac")),
    )
    return jax.shard_map(
        body, mesh=mesh, in_specs=placed, out_specs=P(("grp", "fac"), None, None), check_vma=False
    )
```

```python
import functools
import math

import jax
import jax.numpy as jnp
import numpy as np
from jax import lax
from jax.experimental import pallas as pl
from jax.experimental.pallas import tpu as pltpu
from jax.sharding import PartitionSpec as P

SUB = 64
HALF = SUB // 2
LAYERS = 2
BL_DEV = 4
GROUP = 16
META = 128
PITCH = 40
MESH = pl.DeviceIdType.MESH


def fold_blocks(model_blocks):
    blocks = model_blocks.shape[0]
    pixels = model_blocks.reshape(blocks * LAYERS * 2 * SUB, SUB)
    fold = np.zeros((SUB, SUB), np.float32)
    for n in range(HALF):
        fold[HALF + n, n] = fold[HALF - 1 - n, n] = 1.0
        fold[HALF + n, HALF + n], fold[HALF - 1 - n, HALF + n] = 1.0, -1.0
    fold = jnp.asarray(fold, jnp.bfloat16)
    x = jnp.dot(pixels, fold, preferred_element_type=jnp.float32)
    x = x.reshape(blocks, LAYERS, 2, SUB, SUB)
    plus, minus = x[:, 0] + x[:, 1], x[:, 0] - x[:, 1]
    x = jnp.stack([plus, minus], axis=1)
    upper, lower = x[:, :, :, HALF:], x[:, :, :, HALF - 1 :: -1]
    even, odd = upper + lower, upper - lower

    def parts(rows, turn):
        out_re, out_im = [], []
        for k in range(2):
            for m in range(2):
                re = rows[:, k, 0, :, m * HALF : (m + 1) * HALF]
                im = rows[:, k, 1, :, m * HALF : (m + 1) * HALF]
                times = (k - m + turn) % 4
                for _ in range(times):
                    re, im = -im, re
                out_re.append(re)
                out_im.append(im)
        return jnp.concatenate(out_re, axis=2), jnp.concatenate(out_im, axis=2)

    even_re, even_im = parts(even, 0)
    odd_re, odd_im = parts(odd, 3)
    return jnp.concatenate([even_re, even_im, odd_re, odd_im], axis=1).astype(jnp.bfloat16)


def sincos(x):
    n = jnp.floor(x + 0.5)
    t = (x - n) * (0.5 * math.pi)
    t2 = t * t
    s = t * (1.0 + t2 * (-1.0 / 6 + t2 * (1.0 / 120 + t2 * (-1.0 / 5040 + t2 * (1.0 / 362880)))))
    c = 1.0 + t2 * (-0.5 + t2 * (1.0 / 24 + t2 * (-1.0 / 720 + t2 * (1.0 / 40320 - t2 * (1.0 / 3628800)))))
    turn = n.astype(jnp.int32)
    swap = (turn & 1) == 1
    sine = jnp.where(swap, c, s)
    cosine = jnp.where(swap, s, c)
    sine = jnp.where((turn & 2) == 2, -sine, sine)
    cosine = jnp.where(((turn + 1) & 2) == 2, -cosine, cosine)
    return sine, cosine


def powers(x, cos_ref, sin_ref):
    s0, c0 = sincos(0.5 * x)
    s1, c1 = 2.0 * s0 * c0, 1.0 - 2.0 * s0 * s0
    s, c = s0, c0
    lanes = x.shape[1] // 128
    for p in range(HALF):
        for a in range(lanes):
            cos_ref[a, pl.ds(p, GROUP, stride=PITCH), :] = c[:, a * 128 : (a + 1) * 128]
            sin_ref[a, pl.ds(p, GROUP, stride=PITCH), :] = s[:, a * 128 : (a + 1) * 128]
        if p < HALF - 1:
            s, c = s * c1 + c * s1, c * c1 - s * s1
    return s0, c0


def load(ref, t):
    lanes = ref.shape[0]
    return jnp.concatenate([ref[a, pl.ds(t * PITCH, HALF), :] for a in range(lanes)], axis=1)


def compute_kernel(block_ids, baselines, slots_ref, folded_ref, out_ref, ru, su, rv, sv, cw_ref, sw_ref, sums):
    g = pl.program_id(0)
    vis = out_ref.shape[1] // 2

    @pl.when(g == 0)
    def _():
        out_ref[...] = jnp.zeros_like(out_ref)

    u, v, w = (slots_ref[:, i * vis : (i + 1) * vis] for i in range(3))
    us, uc = powers(u, ru, su)
    vs, vc = powers(v, rv, sv)
    ws, wc = sincos(2.0 * w)
    cw_ref[...] = wc
    sw_ref[...] = ws
    for t in range(GROUP):
        c, s = load(rv, t), load(sv, t)
        cw, sw = cw_ref[t : t + 1, :], sw_ref[t : t + 1, :]
        basis = jnp.concatenate([c * cw, s * cw, c * sw, s * sw], axis=0).astype(jnp.bfloat16)
        inner = jnp.dot(folded_ref[block_ids[g * GROUP + t]], basis, preferred_element_type=jnp.float32)
        rc, rs = load(ru, t), load(su, t)
        re = jnp.sum(rc * inner[:HALF] + rs * inner[2 * HALF : 3 * HALF], axis=0, keepdims=True)
        im = jnp.sum(rc * inner[HALF : 2 * HALF] + rs * inner[3 * HALF :], axis=0, keepdims=True)
        sums[t : t + 1, :vis] = re
        sums[t : t + 1, vis:] = im
    hc, hs = uc * vc - us * vs, uc * vs + us * vc
    re, im = sums[:, :vis], sums[:, vis:]
    live = lax.broadcasted_iota(jnp.int32, (GROUP, vis), 1).astype(jnp.float32) < slots_ref[:, 3 * vis : 3 * vis + 1]
    sums[:, :vis] = jnp.where(live, re * hc - im * hs, 0.0)
    sums[:, vis:] = jnp.where(live, re * hs + im * hc, 0.0)
    for t in range(GROUP):
        b = baselines[g * GROUP + t]
        out_ref[pl.ds(b, 1), :] += sums[t : t + 1, :]


def compute(slots, block_ids, baselines, folded, n_baselines, vis):
    n, width = slots.shape
    lanes = vis // 128
    table = pltpu.VMEM((lanes, GROUP * PITCH, 128), jnp.float32)
    return pl.pallas_call(
        compute_kernel,
        out_shape=jax.ShapeDtypeStruct((n_baselines, 2 * vis), jnp.float32),
        grid_spec=pltpu.PrefetchScalarGridSpec(
            num_scalar_prefetch=2,
            grid=(n // GROUP,),
            in_specs=[
                pl.BlockSpec((GROUP, width), lambda g, *_: (g, 0)),
                pl.BlockSpec(folded.shape, lambda g, *_: (0, 0, 0)),
            ],
            out_specs=pl.BlockSpec((n_baselines, 2 * vis), lambda g, *_: (0, 0)),
            scratch_shapes=[
                table,
                table,
                table,
                table,
                pltpu.VMEM((GROUP, vis), jnp.float32),
                pltpu.VMEM((GROUP, vis), jnp.float32),
                pltpu.VMEM((GROUP, 2 * vis), jnp.float32),
            ],
        ),
        compiler_params=pltpu.CompilerParams(vmem_limit_bytes=32 * 1024 * 1024),
        cost_estimate=pl.CostEstimate(flops=n * 128 * 128 * 768, bytes_accessed=4 * n * width, transcendentals=0),
    )(block_ids, baselines, slots, folded)


def fold_matrices():
    one = np.zeros((SUB, SUB), np.float32)
    for n in range(HALF):
        one[HALF + n, n] = one[HALF - 1 - n, n] = 1.0
        one[HALF + n, HALF + n], one[HALF - 1 - n, HALF + n] = 1.0, -1.0
    by_layer = []
    for sign in (1.0, -1.0):
        pair = np.concatenate([one, sign * one], axis=1)
        zero = np.zeros_like(pair)
        by_layer.append(np.block([[pair, zero], [zero, pair]]))
    rows = one.T.reshape(SUB, HALF, 2).transpose(0, 2, 1).reshape(SUB, SUB)
    rows = np.concatenate([rows, rows], axis=1)
    return tuple(jnp.asarray(x, jnp.bfloat16) for x in (*by_layer, rows))


def fold_one(pixels, right0, right1, left):
    y = jnp.dot(pixels[:SUB], right0, preferred_element_type=jnp.float32)
    y = y + jnp.dot(pixels[SUB:], right1, preferred_element_type=jnp.float32)
    wide = 2 * SUB
    z = []
    for c in range(2):
        part = y[c * HALF : (c + 1) * HALF]
        part = jnp.concatenate([part[:, :wide], part[:, wide:]], axis=0)
        high = part.astype(jnp.bfloat16)
        low = (part - high.astype(jnp.float32)).astype(jnp.bfloat16)
        z.append(jnp.dot(left, jnp.concatenate([high, low], axis=0), preferred_element_type=jnp.float32))
    re, im = z
    term = lax.broadcasted_iota(jnp.int32, (HALF, wide), 1) // HALF

    def pick(a, b, c, d):
        return jnp.where(term == 0, a, jnp.where(term == 1, b, jnp.where(term == 2, c, d)))

    ere, eim, ore, oim = re[:HALF], im[:HALF], re[HALF:], im[HALF:]
    rows = [
        pick(ere, eim, -eim, ere),
        pick(eim, -ere, ere, eim),
        pick(oim, -ore, ore, oim),
        pick(-ore, -oim, oim, -ore),
    ]
    return jnp.concatenate(rows, axis=0).astype(jnp.bfloat16)


def fused_kernel(
    n, source, coords_ref, meta_ref, blocks_ref, right0, right1, left, out_ref,
    send, recv, meta_recv, meta_smem, folded, ru, su, rv, sv, cw_ref, sw_ref, sums, partial, shares,
    send_sem, recv_sem, meta_send, meta_got, share_send, share_got, local_sem,
):
    vis = coords_ref.shape[2]
    me = lax.axis_index("fac")
    barrier = pltpu.get_barrier_semaphore()

    def peer_of(d):
        return lax.rem(me + d, n)

    @pl.loop(1, n)
    def _(d):
        pl.semaphore_signal(barrier, inc=1, device_id={"fac": peer_of(d)}, device_id_type=MESH)

    def pack(d, to):
        peer = peer_of(d)
        for r in range(GROUP):
            row = coords_ref[source[peer * GROUP + r]]
            for i in range(3):
                to[d, i, r : r + 1, :] = row[i : i + 1]

    pack(0, recv)
    meta_recv[0] = meta_ref[me]

    @pl.loop(1, n)
    def _(d):
        pack(d, send)

    pl.semaphore_wait(barrier, n - 1)

    def meta_copy(d):
        return pltpu.make_async_remote_copy(
            src_ref=meta_ref.at[peer_of(d)], dst_ref=meta_recv.at[d], send_sem=meta_send.at[d],
            recv_sem=meta_got.at[d], device_id={"fac": peer_of(d)}, device_id_type=MESH,
        )

    def slot_copy(d):
        return pltpu.make_async_remote_copy(
            src_ref=send.at[d], dst_ref=recv.at[d], send_sem=send_sem.at[d],
            recv_sem=recv_sem.at[d], device_id={"fac": peer_of(d)}, device_id_type=MESH,
        )

    @pl.loop(1, n)
    def _(d):
        meta_copy(d).start()

    @pl.loop(1, n)
    def _(d):
        slot_copy(d).start()

    @pl.loop(0, blocks_ref.shape[0])
    def _(b):
        folded[b] = fold_one(blocks_ref[b], right0[...], right1[...], left[...])

    @pl.loop(1, n)
    def _(d):
        meta_copy(d).wait()

    to_scalars = pltpu.make_async_copy(meta_recv, meta_smem, local_sem)
    to_scalars.start()
    partial[...] = jnp.zeros_like(partial)
    to_scalars.wait()

    @pl.loop(0, n)
    def _(d):
        @pl.when(d > 0)
        def _():
            slot_copy(d).wait()

        us, uc = powers(recv[d, 0], ru, su)
        vs, vc = powers(recv[d, 1], rv, sv)
        ws, wc = sincos(2.0 * recv[d, 2])
        cw_ref[...] = wc
        sw_ref[...] = ws
        for t in range(GROUP):
            c, s = load(rv, t), load(sv, t)
            cw, sw = cw_ref[t : t + 1, :], sw_ref[t : t + 1, :]
            basis = jnp.concatenate([c * cw, s * cw, c * sw, s * sw], axis=0).astype(jnp.bfloat16)
            inner = jnp.dot(folded[meta_smem[d, t, 1]], basis, preferred_element_type=jnp.float32)
            rc, rs = load(ru, t), load(su, t)
            re = jnp.sum(rc * inner[:HALF] + rs * inner[2 * HALF : 3 * HALF], axis=0, keepdims=True)
            im = jnp.sum(rc * inner[HALF : 2 * HALF] + rs * inner[3 * HALF :], axis=0, keepdims=True)
            sums[t : t + 1, :vis] = re
            sums[t : t + 1, vis:] = im
        hc, hs = uc * vc - us * vs, uc * vs + us * vc
        re, im = sums[:, :vis], sums[:, vis:]
        meta = meta_recv[d]
        live = lax.broadcasted_iota(jnp.int32, (GROUP, vis), 1) < meta[:, 0:1]
        both = jnp.concatenate([re * hc - im * hs, re * hs + im * hc], axis=0)
        both = jnp.where(jnp.concatenate([live, live], axis=0), both, 0.0)
        high = both.astype(jnp.bfloat16).astype(jnp.float32)
        both = jnp.concatenate([high, both - high], axis=0).astype(jnp.bfloat16)
        baseline = meta[:, 2:3]
        row = (baseline // BL_DEV) * (2 * BL_DEV) + baseline % BL_DEV
        row = jnp.concatenate([row, row + BL_DEV, row, row + BL_DEV], axis=0)
        onehot = lax.broadcasted_iota(jnp.int32, (4 * GROUP, n * 2 * BL_DEV), 1) == row
        onehot = jnp.where(onehot, 1.0, 0.0).astype(jnp.bfloat16)
        added = lax.dot_general(onehot, both, (((0,), (0,)), ((), ())), preferred_element_type=jnp.float32)
        partial[...] += added.reshape(partial.shape)

    def share_copy(d):
        return pltpu.make_async_remote_copy(
            src_ref=partial.at[peer_of(d)], dst_ref=shares.at[d], send_sem=share_send.at[d],
            recv_sem=share_got.at[d], device_id={"fac": peer_of(d)}, device_id_type=MESH,
        )

    @pl.loop(1, n)
    def _(d):
        share_copy(d).start()

    out_ref[...] = partial[me]

    @pl.loop(1, n)
    def _(d):
        share_copy(d).wait()
        out_ref[...] += shares[d]


def fused(source, coords, meta, blocks, n):
    tasks, _, vis = coords.shape
    table = pltpu.VMEM((vis // 128, GROUP * PITCH, 128), jnp.float32)
    vmem = pl.BlockSpec(memory_space=pltpu.VMEM)
    rows = 2 * BL_DEV
    sems = pltpu.SemaphoreType.DMA((n,))
    return pl.pallas_call(
        functools.partial(fused_kernel, n),
        out_shape=jax.ShapeDtypeStruct((rows, vis), jnp.float32),
        in_specs=[pl.BlockSpec(memory_space=pltpu.SMEM)] + [vmem] * 6,
        out_specs=vmem,
        scratch_shapes=[
            pltpu.VMEM((n, 3, GROUP, vis), jnp.float32),
            pltpu.VMEM((n, 3, GROUP, vis), jnp.float32),
            pltpu.VMEM((n, GROUP, META), jnp.int32),
            pltpu.SMEM((n, GROUP, META), jnp.int32),
            pltpu.VMEM((blocks.shape[0], 2 * SUB, 2 * SUB), jnp.bfloat16),
            table,
            table,
            table,
            table,
            pltpu.VMEM((GROUP, vis), jnp.float32),
            pltpu.VMEM((GROUP, vis), jnp.float32),
            pltpu.VMEM((GROUP, 2 * vis), jnp.float32),
            pltpu.VMEM((n, rows, vis), jnp.float32),
            pltpu.VMEM((n, rows, vis), jnp.float32),
            sems,
            sems,
            sems,
            sems,
            sems,
            sems,
            pltpu.SemaphoreType.DMA,
        ],
        compiler_params=pltpu.CompilerParams(
            collective_id=0, has_side_effects=True, vmem_limit_bytes=40 * 1024 * 1024
        ),
        cost_estimate=pl.CostEstimate(
            flops=n * GROUP * 128 * 128 * 768, bytes_accessed=4 * n * GROUP * 3 * vis, transcendentals=0
        ),
    )(source, coords, meta, blocks, *fold_matrices())


def body(model_blocks, task_owner, task_block, baseline_of_task, coords, vis_count):
    facets = lax.axis_size("fac")
    tasks, _, vis = coords.shape
    capacity = max(2, 2 * tasks // facets)
    slots = facets * capacity
    owner = task_owner[:, 0]
    same = owner[:, None] == owner[None, :]
    before = jnp.arange(tasks)[None, :] < jnp.arange(tasks)[:, None]
    rank = jnp.sum((same & before).astype(jnp.int32), axis=1)
    slot = owner * capacity + rank
    hit = jnp.arange(slots, dtype=jnp.int32)[:, None] == slot[None, :]
    source = jnp.sum(jnp.where(hit, jnp.arange(tasks, dtype=jnp.int32)[None, :], 0), axis=1)
    meta = jnp.stack([vis_count, task_block, baseline_of_task], axis=1)
    meta = jnp.sum(jnp.where(hit[:, :, None], meta[None], 0), axis=1)
    meta = jnp.pad(meta, ((0, 0), (0, META - 3)))
    if capacity == GROUP:
        blocks = model_blocks.reshape(model_blocks.shape[0], 2 * SUB, 2 * SUB)
        share = fused(source, coords, meta.reshape(facets, capacity, META), blocks, facets)
        return share.reshape(2, BL_DEV, vis).transpose(1, 0, 2)
    meta = meta.astype(jnp.float32)
    rows = coords.reshape(tasks, 3 * vis)[source]
    sent = jnp.concatenate([rows, meta], axis=1)
    sent = sent.reshape(facets, capacity, 3 * vis + META)
    got = lax.all_to_all(sent, "fac", split_axis=0, concat_axis=0, tiled=True).reshape(slots, 3 * vis + META)
    folded = fold_blocks(model_blocks)
    block_ids = got[:, 3 * vis + 1].astype(jnp.int32)
    baselines = got[:, 3 * vis + 2].astype(jnp.int32)
    partial = compute(got, block_ids, baselines, folded, BL_DEV * facets, vis)
    shares = partial.reshape(facets, BL_DEV, 2 * vis)
    shares = lax.all_to_all(shares, "fac", split_axis=0, concat_axis=0, tiled=True)
    return jnp.sum(shares, axis=0).reshape(BL_DEV, 2, vis)


def solution(mesh):
    placed = (
        P(("grp", "fac"), None),
        P(("grp", "fac"), None),
        P(("grp", "fac")),
        P(("grp", "fac")),
        P(("grp", "fac"), None, None),
        P(("grp", "fac")),
    )
    return jax.shard_map(
        body, mesh=mesh, in_specs=placed, out_specs=P(("grp", "fac"), None, None), check_vma=False
    )
```

```python
import functools
import math

import jax
import jax.numpy as jnp
import numpy as np
from jax import lax
from jax.experimental import pallas as pl
from jax.experimental.pallas import tpu as pltpu
from jax.sharding import PartitionSpec as P

SUB = 64
HALF = SUB // 2
LAYERS = 2
BL_DEV = 4
GROUP = 16
META = 128
PITCH = 40
STEPS = 16383.5
MESH = pl.DeviceIdType.MESH


def fold_blocks(model_blocks):
    blocks = model_blocks.shape[0]
    pixels = model_blocks.reshape(blocks * LAYERS * 2 * SUB, SUB)
    fold = np.zeros((SUB, SUB), np.float32)
    for n in range(HALF):
        fold[HALF + n, n] = fold[HALF - 1 - n, n] = 1.0
        fold[HALF + n, HALF + n], fold[HALF - 1 - n, HALF + n] = 1.0, -1.0
    fold = jnp.asarray(fold, jnp.bfloat16)
    x = jnp.dot(pixels, fold, preferred_element_type=jnp.float32)
    x = x.reshape(blocks, LAYERS, 2, SUB, SUB)
    plus, minus = x[:, 0] + x[:, 1], x[:, 0] - x[:, 1]
    x = jnp.stack([plus, minus], axis=1)
    upper, lower = x[:, :, :, HALF:], x[:, :, :, HALF - 1 :: -1]
    even, odd = upper + lower, upper - lower

    def parts(rows, turn):
        out_re, out_im = [], []
        for k in range(2):
            for m in range(2):
                re = rows[:, k, 0, :, m * HALF : (m + 1) * HALF]
                im = rows[:, k, 1, :, m * HALF : (m + 1) * HALF]
                times = (k - m + turn) % 4
                for _ in range(times):
                    re, im = -im, re
                out_re.append(re)
                out_im.append(im)
        return jnp.concatenate(out_re, axis=2), jnp.concatenate(out_im, axis=2)

    even_re, even_im = parts(even, 0)
    odd_re, odd_im = parts(odd, 3)
    return jnp.concatenate([even_re, even_im, odd_re, odd_im], axis=1).astype(jnp.bfloat16)


def sincos(x):
    n = jnp.floor(x + 0.5)
    t = (x - n) * (0.5 * math.pi)
    t2 = t * t
    s = t * (1.0 + t2 * (-1.0 / 6 + t2 * (1.0 / 120 + t2 * (-1.0 / 5040 + t2 * (1.0 / 362880)))))
    c = 1.0 + t2 * (-0.5 + t2 * (1.0 / 24 + t2 * (-1.0 / 720 + t2 * (1.0 / 40320 - t2 * (1.0 / 3628800)))))
    turn = n.astype(jnp.int32)
    swap = (turn & 1) == 1
    sine = jnp.where(swap, c, s)
    cosine = jnp.where(swap, s, c)
    sine = jnp.where((turn & 2) == 2, -sine, sine)
    cosine = jnp.where(((turn + 1) & 2) == 2, -cosine, cosine)
    return sine, cosine


def powers(x, cos_ref, sin_ref):
    s0, c0 = sincos(0.5 * x)
    twice = 2.0 - 4.0 * s0 * s0
    s, c, s_last, c_last = s0, c0, -s0, c0
    lanes = x.shape[1] // 128
    for p in range(HALF):
        for a in range(lanes):
            cos_ref[a, pl.ds(p, GROUP, stride=PITCH), :] = c[:, a * 128 : (a + 1) * 128]
            sin_ref[a, pl.ds(p, GROUP, stride=PITCH), :] = s[:, a * 128 : (a + 1) * 128]
        if p < HALF - 1:
            s, c, s_last, c_last = twice * s - s_last, twice * c - c_last, s, c
    return s0, c0


def load(ref, t):
    lanes = ref.shape[0]
    return jnp.concatenate([ref[a, pl.ds(t * PITCH, HALF), :] for a in range(lanes)], axis=1)


def compute_kernel(block_ids, baselines, slots_ref, folded_ref, out_ref, ru, su, rv, sv, cw_ref, sw_ref, sums):
    g = pl.program_id(0)
    vis = out_ref.shape[1] // 2

    @pl.when(g == 0)
    def _():
        out_ref[...] = jnp.zeros_like(out_ref)

    u, v, w = (slots_ref[:, i * vis : (i + 1) * vis] for i in range(3))
    us, uc = powers(u, ru, su)
    vs, vc = powers(v, rv, sv)
    ws, wc = sincos(2.0 * w)
    cw_ref[...] = wc
    sw_ref[...] = ws
    for t in range(GROUP):
        c, s = load(rv, t), load(sv, t)
        cw, sw = cw_ref[t : t + 1, :], sw_ref[t : t + 1, :]
        basis = jnp.concatenate([c * cw, s * cw, c * sw, s * sw], axis=0).astype(jnp.bfloat16)
        inner = jnp.dot(folded_ref[block_ids[g * GROUP + t]], basis, preferred_element_type=jnp.float32)
        rc, rs = load(ru, t), load(su, t)
        re = jnp.sum(rc * inner[:HALF] + rs * inner[2 * HALF : 3 * HALF], axis=0, keepdims=True)
        im = jnp.sum(rc * inner[HALF : 2 * HALF] + rs * inner[3 * HALF :], axis=0, keepdims=True)
        sums[t : t + 1, :vis] = re
        sums[t : t + 1, vis:] = im
    hc, hs = uc * vc - us * vs, uc * vs + us * vc
    re, im = sums[:, :vis], sums[:, vis:]
    live = lax.broadcasted_iota(jnp.int32, (GROUP, vis), 1).astype(jnp.float32) < slots_ref[:, 3 * vis : 3 * vis + 1]
    sums[:, :vis] = jnp.where(live, re * hc - im * hs, 0.0)
    sums[:, vis:] = jnp.where(live, re * hs + im * hc, 0.0)
    for t in range(GROUP):
        b = baselines[g * GROUP + t]
        out_ref[pl.ds(b, 1), :] += sums[t : t + 1, :]


def compute(slots, block_ids, baselines, folded, n_baselines, vis):
    n, width = slots.shape
    lanes = vis // 128
    table = pltpu.VMEM((lanes, GROUP * PITCH, 128), jnp.float32)
    return pl.pallas_call(
        compute_kernel,
        out_shape=jax.ShapeDtypeStruct((n_baselines, 2 * vis), jnp.float32),
        grid_spec=pltpu.PrefetchScalarGridSpec(
            num_scalar_prefetch=2,
            grid=(n // GROUP,),
            in_specs=[
                pl.BlockSpec((GROUP, width), lambda g, *_: (g, 0)),
                pl.BlockSpec(folded.shape, lambda g, *_: (0, 0, 0)),
            ],
            out_specs=pl.BlockSpec((n_baselines, 2 * vis), lambda g, *_: (0, 0)),
            scratch_shapes=[
                table,
                table,
                table,
                table,
                pltpu.VMEM((GROUP, vis), jnp.float32),
                pltpu.VMEM((GROUP, vis), jnp.float32),
                pltpu.VMEM((GROUP, 2 * vis), jnp.float32),
            ],
        ),
        compiler_params=pltpu.CompilerParams(vmem_limit_bytes=32 * 1024 * 1024),
        cost_estimate=pl.CostEstimate(flops=n * 128 * 128 * 768, bytes_accessed=4 * n * width, transcendentals=0),
    )(block_ids, baselines, slots, folded)


def fold_matrices():
    one = np.zeros((SUB, SUB), np.float32)
    for n in range(HALF):
        one[HALF + n, n] = one[HALF - 1 - n, n] = 1.0
        one[HALF + n, HALF + n], one[HALF - 1 - n, HALF + n] = 1.0, -1.0
    by_layer = []
    for sign in (1.0, -1.0):
        pair = np.concatenate([one, sign * one], axis=1)
        zero = np.zeros_like(pair)
        by_layer.append(np.block([[pair, zero], [zero, pair]]))
    rows = one.T.reshape(SUB, HALF, 2).transpose(0, 2, 1).reshape(SUB, SUB)
    rows = np.concatenate([rows, rows], axis=1)
    return tuple(jnp.asarray(x, jnp.bfloat16) for x in (*by_layer, rows))


def fold_one(pixels, right0, right1, left):
    y = jnp.dot(pixels[:SUB], right0, preferred_element_type=jnp.float32)
    y = y + jnp.dot(pixels[SUB:], right1, preferred_element_type=jnp.float32)
    wide = 2 * SUB
    z = []
    for c in range(2):
        part = y[c * HALF : (c + 1) * HALF]
        part = jnp.concatenate([part[:, :wide], part[:, wide:]], axis=0)
        high = part.astype(jnp.bfloat16)
        low = (part - high.astype(jnp.float32)).astype(jnp.bfloat16)
        z.append(jnp.dot(left, jnp.concatenate([high, low], axis=0), preferred_element_type=jnp.float32))
    re, im = z
    term = lax.broadcasted_iota(jnp.int32, (HALF, wide), 1) // HALF

    def pick(a, b, c, d):
        return jnp.where(term == 0, a, jnp.where(term == 1, b, jnp.where(term == 2, c, d)))

    ere, eim, ore, oim = re[:HALF], im[:HALF], re[HALF:], im[HALF:]
    rows = [
        pick(ere, eim, -eim, ere),
        pick(eim, -ere, ere, eim),
        pick(oim, -ore, ore, oim),
        pick(-ore, -oim, oim, -ore),
    ]
    return jnp.concatenate(rows, axis=0).astype(jnp.bfloat16)


def fused_kernel(
    n, source, coords_ref, meta_ref, blocks_ref, right0, right1, left, out_ref,
    stage, send, recv, meta_recv, meta_smem, folded, ru, su, rv, sv, cw_ref, sw_ref, sums, partial, shares,
    send_sem, recv_sem, meta_send, meta_got, share_send, share_got, local_sem,
):
    vis = coords_ref.shape[2]
    meta_lane = lax.broadcasted_iota(jnp.int32, (GROUP, META), 1)
    meta_row = lax.broadcasted_iota(jnp.int32, (GROUP, META), 0)
    me = lax.axis_index("fac")
    barrier = pltpu.get_barrier_semaphore()

    def peer_of(d):
        return lax.rem(me + d, n)

    @pl.loop(1, n)
    def _(d):
        pl.semaphore_signal(barrier, inc=1, device_id={"fac": peer_of(d)}, device_id_type=MESH)

    def pack(d, to):
        peer = peer_of(d)
        for r in range(GROUP):
            task = source[peer * GROUP + r]
            for i in range(3):
                stage[i, r : r + 1, :] = coords_ref[i, pl.ds(task, 1), :]
        to[d] = jnp.floor(stage[...] * STEPS + 0.5).astype(jnp.int32).astype(jnp.int16)

    pack(0, recv)
    meta_recv[0] = meta_ref[me]

    def meta_copy(d):
        return pltpu.make_async_remote_copy(
            src_ref=meta_ref.at[peer_of(d)], dst_ref=meta_recv.at[d], send_sem=meta_send.at[d],
            recv_sem=meta_got.at[d], device_id={"fac": peer_of(d)}, device_id_type=MESH,
        )

    def slot_copy(d):
        return pltpu.make_async_remote_copy(
            src_ref=send.at[d], dst_ref=recv.at[d], send_sem=send_sem.at[d],
            recv_sem=recv_sem.at[d], device_id={"fac": peer_of(d)}, device_id_type=MESH,
        )

    pl.semaphore_wait(barrier, n - 1)

    @pl.loop(1, n)
    def _(d):
        meta_copy(d).start()

    @pl.loop(1, n)
    def _(d):
        pack(d, send)
        slot_copy(d).start()

    @pl.loop(0, blocks_ref.shape[0])
    def _(b):
        folded[b] = fold_one(blocks_ref[b], right0[...], right1[...], left[...])

    @pl.loop(1, n)
    def _(d):
        meta_copy(d).wait()

    to_scalars = pltpu.make_async_copy(meta_recv, meta_smem, local_sem)
    to_scalars.start()
    partial[...] = jnp.zeros_like(partial)
    to_scalars.wait()

    @pl.loop(0, n)
    def _(d):
        @pl.when(d > 0)
        def _():
            slot_copy(d).wait()

        u, v, w = (recv[d, i].astype(jnp.int32).astype(jnp.float32) * (1.0 / STEPS) for i in range(3))
        us, uc = powers(u, ru, su)
        vs, vc = powers(v, rv, sv)
        ws, wc = sincos(2.0 * w)
        cw_ref[...] = wc
        sw_ref[...] = ws
        for t in range(GROUP):
            c, s = load(rv, t), load(sv, t)
            cw, sw = cw_ref[t : t + 1, :], sw_ref[t : t + 1, :]
            basis = jnp.concatenate([c * cw, s * cw, c * sw, s * sw], axis=0).astype(jnp.bfloat16)
            inner = jnp.dot(folded[meta_smem[d, 0, GROUP + t]], basis, preferred_element_type=jnp.float32)
            rc, rs = load(ru, t), load(su, t)
            re = jnp.sum(rc * inner[:HALF] + rs * inner[2 * HALF : 3 * HALF], axis=0, keepdims=True)
            im = jnp.sum(rc * inner[HALF : 2 * HALF] + rs * inner[3 * HALF :], axis=0, keepdims=True)
            sums[t : t + 1, :vis] = re
            sums[t : t + 1, vis:] = im
        hc, hs = uc * vc - us * vs, uc * vs + us * vc
        re, im = sums[:, :vis], sums[:, vis:]
        meta = meta_recv[d].astype(jnp.float32)

        def column(first):
            picked = jnp.where(meta_lane == meta_row + first, meta, 0.0)
            return jnp.sum(picked, axis=1, keepdims=True)

        live = lax.broadcasted_iota(jnp.int32, (GROUP, vis), 1).astype(jnp.float32) < column(0)
        both = jnp.concatenate([re * hc - im * hs, re * hs + im * hc], axis=0)
        both = jnp.where(jnp.concatenate([live, live], axis=0), both, 0.0)
        high = both.astype(jnp.bfloat16).astype(jnp.float32)
        both = jnp.concatenate([high, both - high], axis=0).astype(jnp.bfloat16)
        row = column(2 * GROUP)
        row = jnp.concatenate([row, row + BL_DEV, row, row + BL_DEV], axis=0)
        onehot = lax.broadcasted_iota(jnp.int32, (4 * GROUP, n * 2 * BL_DEV), 1).astype(jnp.float32) == row
        onehot = jnp.where(onehot, 1.0, 0.0).astype(jnp.bfloat16)
        added = lax.dot_general(onehot, both, (((0,), (0,)), ((), ())), preferred_element_type=jnp.float32)
        partial[...] += added.reshape(partial.shape)

    def share_copy(d):
        return pltpu.make_async_remote_copy(
            src_ref=partial.at[peer_of(d)], dst_ref=shares.at[d], send_sem=share_send.at[d],
            recv_sem=share_got.at[d], device_id={"fac": peer_of(d)}, device_id_type=MESH,
        )

    @pl.loop(1, n)
    def _(d):
        share_copy(d).start()

    out_ref[...] = partial[me]

    @pl.loop(1, n)
    def _(d):
        share_copy(d).wait()
        out_ref[...] += shares[d]


def fused(source, coords, meta, blocks, n):
    vis = coords.shape[2]
    table = pltpu.VMEM((vis // 128, GROUP * PITCH, 128), jnp.float32)
    vmem = pl.BlockSpec(memory_space=pltpu.VMEM)
    rows = 2 * BL_DEV
    sems = pltpu.SemaphoreType.DMA((n,))
    return pl.pallas_call(
        functools.partial(fused_kernel, n),
        out_shape=jax.ShapeDtypeStruct((rows, vis), jnp.float32),
        in_specs=[pl.BlockSpec(memory_space=pltpu.SMEM)] + [vmem] * 6,
        out_specs=vmem,
        scratch_shapes=[
            pltpu.VMEM((3, GROUP, vis), jnp.float32),
            pltpu.VMEM((n, 3, GROUP, vis), jnp.int16),
            pltpu.VMEM((n, 3, GROUP, vis), jnp.int16),
            pltpu.VMEM((n, 1, META), jnp.int32),
            pltpu.SMEM((n, 1, META), jnp.int32),
            pltpu.VMEM((blocks.shape[0], 2 * SUB, 2 * SUB), jnp.bfloat16),
            table,
            table,
            table,
            table,
            pltpu.VMEM((GROUP, vis), jnp.float32),
            pltpu.VMEM((GROUP, vis), jnp.float32),
            pltpu.VMEM((GROUP, 2 * vis), jnp.float32),
            pltpu.VMEM((n, rows, vis), jnp.float32),
            pltpu.VMEM((n, rows, vis), jnp.float32),
            sems,
            sems,
            sems,
            sems,
            sems,
            sems,
            pltpu.SemaphoreType.DMA,
        ],
        compiler_params=pltpu.CompilerParams(
            collective_id=0, has_side_effects=True, vmem_limit_bytes=40 * 1024 * 1024
        ),
        cost_estimate=pl.CostEstimate(
            flops=n * GROUP * 128 * 128 * 768, bytes_accessed=4 * n * GROUP * 3 * vis, transcendentals=0
        ),
    )(source, coords, meta, blocks, *fold_matrices())


def body(model_blocks, task_owner, task_block, baseline_of_task, coords, vis_count):
    facets = lax.axis_size("fac")
    tasks, _, vis = coords.shape
    capacity = max(2, 2 * tasks // facets)
    slots = facets * capacity
    owner = task_owner[:, 0]
    same = owner[:, None] == owner[None, :]
    before = jnp.arange(tasks)[None, :] < jnp.arange(tasks)[:, None]
    rank = jnp.sum((same & before).astype(jnp.int32), axis=1)
    slot = owner * capacity + rank
    hit = jnp.arange(slots, dtype=jnp.int32)[:, None] == slot[None, :]
    source = jnp.sum(jnp.where(hit, jnp.arange(tasks, dtype=jnp.int32)[None, :], 0), axis=1)
    if capacity == GROUP:
        row = (baseline_of_task // BL_DEV) * (2 * BL_DEV) + baseline_of_task % BL_DEV
        meta = jnp.stack([vis_count, task_block, row])
        meta = jnp.where(hit.reshape(facets, 1, capacity, tasks), meta[None, :, None, :], 0)
        meta = jnp.sum(meta, axis=3).reshape(facets, 1, 3 * capacity)
        meta = jnp.pad(meta, ((0, 0), (0, 0), (0, META - 3 * capacity)))
        blocks = model_blocks.reshape(model_blocks.shape[0], 2 * SUB, 2 * SUB)
        share = fused(source, coords.transpose(1, 0, 2), meta, blocks, facets)
        return share.reshape(2, BL_DEV, vis).transpose(1, 0, 2)
    meta = jnp.stack([vis_count, task_block, baseline_of_task], axis=1)
    meta = jnp.sum(jnp.where(hit[:, :, None], meta[None], 0), axis=1)
    meta = jnp.pad(meta, ((0, 0), (0, META - 3)))
    meta = meta.astype(jnp.float32)
    rows = coords.reshape(tasks, 3 * vis)[source]
    sent = jnp.concatenate([rows, meta], axis=1)
    sent = sent.reshape(facets, capacity, 3 * vis + META)
    got = lax.all_to_all(sent, "fac", split_axis=0, concat_axis=0, tiled=True).reshape(slots, 3 * vis + META)
    folded = fold_blocks(model_blocks)
    block_ids = got[:, 3 * vis + 1].astype(jnp.int32)
    baselines = got[:, 3 * vis + 2].astype(jnp.int32)
    partial = compute(got, block_ids, baselines, folded, BL_DEV * facets, vis)
    shares = partial.reshape(facets, BL_DEV, 2 * vis)
    shares = lax.all_to_all(shares, "fac", split_axis=0, concat_axis=0, tiled=True)
    return jnp.sum(shares, axis=0).reshape(BL_DEV, 2, vis)


def solution(mesh):
    placed = (
        P(("grp", "fac"), None),
        P(("grp", "fac"), None),
        P(("grp", "fac")),
        P(("grp", "fac")),
        P(("grp", "fac"), None, None),
        P(("grp", "fac")),
    )
    return jax.shard_map(
        body, mesh=mesh, in_specs=placed, out_specs=P(("grp", "fac"), None, None), check_vma=False
    )
```

```python
import functools
import math

import jax
import jax.numpy as jnp
import numpy as np
from jax import lax
from jax.experimental import pallas as pl
from jax.experimental.pallas import tpu as pltpu
from jax.sharding import PartitionSpec as P

SUB = 64
HALF = SUB // 2
LAYERS = 2
BL_DEV = 4
GROUP = 16
META = 128
PITCH = 40
STEPS = 16383.5
MESH = pl.DeviceIdType.MESH


def fold_blocks(model_blocks):
    blocks = model_blocks.shape[0]
    pixels = model_blocks.reshape(blocks * LAYERS * 2 * SUB, SUB)
    fold = np.zeros((SUB, SUB), np.float32)
    for n in range(HALF):
        fold[HALF + n, n] = fold[HALF - 1 - n, n] = 1.0
        fold[HALF + n, HALF + n], fold[HALF - 1 - n, HALF + n] = 1.0, -1.0
    fold = jnp.asarray(fold, jnp.bfloat16)
    x = jnp.dot(pixels, fold, preferred_element_type=jnp.float32)
    x = x.reshape(blocks, LAYERS, 2, SUB, SUB)
    plus, minus = x[:, 0] + x[:, 1], x[:, 0] - x[:, 1]
    x = jnp.stack([plus, minus], axis=1)
    upper, lower = x[:, :, :, HALF:], x[:, :, :, HALF - 1 :: -1]
    even, odd = upper + lower, upper - lower

    def parts(rows, turn):
        out_re, out_im = [], []
        for k in range(2):
            for m in range(2):
                re = rows[:, k, 0, :, m * HALF : (m + 1) * HALF]
                im = rows[:, k, 1, :, m * HALF : (m + 1) * HALF]
                times = (k - m + turn) % 4
                for _ in range(times):
                    re, im = -im, re
                out_re.append(re)
                out_im.append(im)
        return jnp.concatenate(out_re, axis=2), jnp.concatenate(out_im, axis=2)

    even_re, even_im = parts(even, 0)
    odd_re, odd_im = parts(odd, 3)
    return jnp.concatenate([even_re, even_im, odd_re, odd_im], axis=1).astype(jnp.bfloat16)


def sincos(x):
    n = jnp.floor(x + 0.5)
    t = (x - n) * (0.5 * math.pi)
    t2 = t * t
    s = t * (1.0 + t2 * (-1.0 / 6 + t2 * (1.0 / 120 + t2 * (-1.0 / 5040 + t2 * (1.0 / 362880)))))
    c = 1.0 + t2 * (-0.5 + t2 * (1.0 / 24 + t2 * (-1.0 / 720 + t2 * (1.0 / 40320 - t2 * (1.0 / 3628800)))))
    turn = n.astype(jnp.int32)
    swap = (turn & 1) == 1
    sine = jnp.where(swap, c, s)
    cosine = jnp.where(swap, s, c)
    sine = jnp.where((turn & 2) == 2, -sine, sine)
    cosine = jnp.where(((turn + 1) & 2) == 2, -cosine, cosine)
    return sine, cosine


def powers(x, cos_ref, sin_ref):
    s0, c0 = sincos(0.5 * x)
    twice = 2.0 - 4.0 * s0 * s0
    s, c, s_last, c_last = s0, c0, -s0, c0
    lanes = x.shape[1] // 128
    for p in range(HALF):
        for a in range(lanes):
            cos_ref[a, pl.ds(p, GROUP, stride=PITCH), :] = c[:, a * 128 : (a + 1) * 128]
            sin_ref[a, pl.ds(p, GROUP, stride=PITCH), :] = s[:, a * 128 : (a + 1) * 128]
        if p < HALF - 1:
            s, c, s_last, c_last = twice * s - s_last, twice * c - c_last, s, c
    return s0, c0


def load(ref, t):
    lanes = ref.shape[0]
    return jnp.concatenate([ref[a, pl.ds(t * PITCH, HALF), :] for a in range(lanes)], axis=1)


def compute_kernel(block_ids, baselines, slots_ref, folded_ref, out_ref, ru, su, rv, sv, cw_ref, sw_ref, sums):
    g = pl.program_id(0)
    vis = out_ref.shape[1] // 2

    @pl.when(g == 0)
    def _():
        out_ref[...] = jnp.zeros_like(out_ref)

    u, v, w = (slots_ref[:, i * vis : (i + 1) * vis] for i in range(3))
    us, uc = powers(u, ru, su)
    vs, vc = powers(v, rv, sv)
    ws, wc = sincos(2.0 * w)
    cw_ref[...] = wc
    sw_ref[...] = ws
    for t in range(GROUP):
        c, s = load(rv, t), load(sv, t)
        cw, sw = cw_ref[t : t + 1, :], sw_ref[t : t + 1, :]
        basis = jnp.concatenate([c * cw, s * cw, c * sw, s * sw], axis=0).astype(jnp.bfloat16)
        inner = jnp.dot(folded_ref[block_ids[g * GROUP + t]], basis, preferred_element_type=jnp.float32)
        rc, rs = load(ru, t), load(su, t)
        re = jnp.sum(rc * inner[:HALF] + rs * inner[2 * HALF : 3 * HALF], axis=0, keepdims=True)
        im = jnp.sum(rc * inner[HALF : 2 * HALF] + rs * inner[3 * HALF :], axis=0, keepdims=True)
        sums[t : t + 1, :vis] = re
        sums[t : t + 1, vis:] = im
    hc, hs = uc * vc - us * vs, uc * vs + us * vc
    re, im = sums[:, :vis], sums[:, vis:]
    live = lax.broadcasted_iota(jnp.int32, (GROUP, vis), 1).astype(jnp.float32) < slots_ref[:, 3 * vis : 3 * vis + 1]
    sums[:, :vis] = jnp.where(live, re * hc - im * hs, 0.0)
    sums[:, vis:] = jnp.where(live, re * hs + im * hc, 0.0)
    for t in range(GROUP):
        b = baselines[g * GROUP + t]
        out_ref[pl.ds(b, 1), :] += sums[t : t + 1, :]


def compute(slots, block_ids, baselines, folded, n_baselines, vis):
    n, width = slots.shape
    lanes = vis // 128
    table = pltpu.VMEM((lanes, GROUP * PITCH, 128), jnp.float32)
    return pl.pallas_call(
        compute_kernel,
        out_shape=jax.ShapeDtypeStruct((n_baselines, 2 * vis), jnp.float32),
        grid_spec=pltpu.PrefetchScalarGridSpec(
            num_scalar_prefetch=2,
            grid=(n // GROUP,),
            in_specs=[
                pl.BlockSpec((GROUP, width), lambda g, *_: (g, 0)),
                pl.BlockSpec(folded.shape, lambda g, *_: (0, 0, 0)),
            ],
            out_specs=pl.BlockSpec((n_baselines, 2 * vis), lambda g, *_: (0, 0)),
            scratch_shapes=[
                table,
                table,
                table,
                table,
                pltpu.VMEM((GROUP, vis), jnp.float32),
                pltpu.VMEM((GROUP, vis), jnp.float32),
                pltpu.VMEM((GROUP, 2 * vis), jnp.float32),
            ],
        ),
        compiler_params=pltpu.CompilerParams(vmem_limit_bytes=32 * 1024 * 1024),
        cost_estimate=pl.CostEstimate(flops=n * 128 * 128 * 768, bytes_accessed=4 * n * width, transcendentals=0),
    )(block_ids, baselines, slots, folded)


def fold_matrices():
    one = np.zeros((SUB, SUB), np.float32)
    for n in range(HALF):
        one[HALF + n, n] = one[HALF - 1 - n, n] = 1.0
        one[HALF + n, HALF + n], one[HALF - 1 - n, HALF + n] = 1.0, -1.0
    by_layer = []
    for sign in (1.0, -1.0):
        pair = np.concatenate([one, sign * one], axis=1)
        zero = np.zeros_like(pair)
        by_layer.append(np.block([[pair, zero], [zero, pair]]))
    rows = one.T.reshape(SUB, HALF, 2).transpose(0, 2, 1).reshape(SUB, SUB)
    rows = np.concatenate([rows, rows], axis=1)
    return tuple(jnp.asarray(x, jnp.bfloat16) for x in (*by_layer, rows))


def fold_one(pixels, right0, right1, left):
    y = jnp.dot(pixels[:SUB], right0, preferred_element_type=jnp.float32)
    y = y + jnp.dot(pixels[SUB:], right1, preferred_element_type=jnp.float32)
    wide = 2 * SUB
    z = []
    for c in range(2):
        part = y[c * HALF : (c + 1) * HALF]
        part = jnp.concatenate([part[:, :wide], part[:, wide:]], axis=0)
        high = part.astype(jnp.bfloat16)
        low = (part - high.astype(jnp.float32)).astype(jnp.bfloat16)
        z.append(jnp.dot(left, jnp.concatenate([high, low], axis=0), preferred_element_type=jnp.float32))
    re, im = z
    term = lax.broadcasted_iota(jnp.int32, (HALF, wide), 1) // HALF

    def pick(a, b, c, d):
        return jnp.where(term == 0, a, jnp.where(term == 1, b, jnp.where(term == 2, c, d)))

    ere, eim, ore, oim = re[:HALF], im[:HALF], re[HALF:], im[HALF:]
    rows = [
        pick(ere, eim, -eim, ere),
        pick(eim, -ere, ere, eim),
        pick(oim, -ore, ore, oim),
        pick(-ore, -oim, oim, -ore),
    ]
    rows = jnp.concatenate(rows, axis=0)
    high = rows.astype(jnp.bfloat16)
    return jnp.concatenate([high, (rows - high.astype(jnp.float32)).astype(jnp.bfloat16)], axis=1)


def fused_kernel(
    n, source, coords_ref, meta_ref, blocks_ref, right0, right1, left, out_ref,
    stage, send, recv, meta_recv, meta_smem, folded, ru, su, rv, sv, cw_ref, sw_ref, sums, partial, shares,
    send_sem, recv_sem, meta_send, meta_got, share_send, share_got, local_sem,
):
    vis = coords_ref.shape[2]
    meta_lane = lax.broadcasted_iota(jnp.int32, (GROUP, META), 1)
    meta_row = lax.broadcasted_iota(jnp.int32, (GROUP, META), 0)
    me = lax.axis_index("fac")
    barrier = pltpu.get_barrier_semaphore()

    def peer_of(d):
        return lax.rem(me + d, n)

    @pl.loop(1, n)
    def _(d):
        pl.semaphore_signal(barrier, inc=1, device_id={"fac": peer_of(d)}, device_id_type=MESH)

    def pack(d, to):
        peer = peer_of(d)
        for r in range(GROUP):
            task = source[peer * GROUP + r]
            for i in range(3):
                stage[i, r : r + 1, :] = coords_ref[i, pl.ds(task, 1), :]
        to[d] = jnp.floor(stage[...] * STEPS + 0.5).astype(jnp.int32).astype(jnp.int16)

    pack(0, recv)
    meta_recv[0] = meta_ref[me]
    partial[...] = jnp.zeros_like(partial)

    @pl.loop(0, blocks_ref.shape[0], step=2)
    def _(b):
        for i in range(2):
            folded[b + i] = fold_one(blocks_ref[b + i], right0[...], right1[...], left[...])


    def meta_copy(d):
        return pltpu.make_async_remote_copy(
            src_ref=meta_ref.at[peer_of(d)], dst_ref=meta_recv.at[d], send_sem=meta_send.at[d],
            recv_sem=meta_got.at[d], device_id={"fac": peer_of(d)}, device_id_type=MESH,
        )

    def slot_copy(d):
        return pltpu.make_async_remote_copy(
            src_ref=send.at[d], dst_ref=recv.at[d], send_sem=send_sem.at[d],
            recv_sem=recv_sem.at[d], device_id={"fac": peer_of(d)}, device_id_type=MESH,
        )

    pl.semaphore_wait(barrier, n - 1)

    @pl.loop(1, n)
    def _(d):
        meta_copy(d).start()

    @pl.loop(1, n)
    def _(d):
        pack(d, send)
        slot_copy(d).start()

    @pl.loop(1, n)
    def _(d):
        meta_copy(d).wait()

    to_scalars = pltpu.make_async_copy(meta_recv, meta_smem, local_sem)
    to_scalars.start()
    to_scalars.wait()

    @pl.loop(0, n)
    def _(d):
        @pl.when(d > 0)
        def _():
            slot_copy(d).wait()

        u, v, w = (recv[d, i].astype(jnp.int32).astype(jnp.float32) * (1.0 / STEPS) for i in range(3))
        us, uc = powers(u, ru, su)
        vs, vc = powers(v, rv, sv)
        ws, wc = sincos(2.0 * w)
        cw_ref[...] = wc
        sw_ref[...] = ws
        for t in range(GROUP):
            c, s = load(rv, t), load(sv, t)
            cw, sw = cw_ref[t : t + 1, :], sw_ref[t : t + 1, :]
            basis = jnp.concatenate([c * cw, s * cw, c * sw, s * sw], axis=0).astype(jnp.bfloat16)
            basis = jnp.concatenate([basis, basis], axis=0)
            inner = jnp.dot(folded[meta_smem[d, 0, GROUP + t]], basis, preferred_element_type=jnp.float32)
            rc, rs = load(ru, t), load(su, t)
            re = jnp.sum(rc * inner[:HALF] + rs * inner[2 * HALF : 3 * HALF], axis=0, keepdims=True)
            im = jnp.sum(rc * inner[HALF : 2 * HALF] + rs * inner[3 * HALF :], axis=0, keepdims=True)
            sums[t : t + 1, :vis] = re
            sums[t : t + 1, vis:] = im
        hc, hs = uc * vc - us * vs, uc * vs + us * vc
        re, im = sums[:, :vis], sums[:, vis:]
        meta = meta_recv[d]
        count = jnp.sum(jnp.where(meta_lane == meta_row, meta.astype(jnp.float32), 0.0), axis=1, keepdims=True)
        live = lax.broadcasted_iota(jnp.int32, (GROUP, vis), 1).astype(jnp.float32) < count
        both = jnp.concatenate([re * hc - im * hs, re * hs + im * hc], axis=0)
        both = jnp.where(jnp.concatenate([live, live], axis=0), both, 0.0)
        high = both.astype(jnp.bfloat16).astype(jnp.float32)
        both = jnp.concatenate([high, both - high], axis=0).astype(jnp.bfloat16)
        onehot = lax.broadcasted_iota(jnp.int32, (n * 2 * BL_DEV, 4 * GROUP), 0) == meta[:, 4 * GROUP :]
        onehot = jnp.where(onehot, 1.0, 0.0).astype(jnp.bfloat16)
        added = jnp.dot(onehot, both, preferred_element_type=jnp.float32)
        partial[...] += added.reshape(partial.shape)

    def share_copy(d):
        return pltpu.make_async_remote_copy(
            src_ref=partial.at[peer_of(d)], dst_ref=shares.at[d], send_sem=share_send.at[d],
            recv_sem=share_got.at[d], device_id={"fac": peer_of(d)}, device_id_type=MESH,
        )

    @pl.loop(1, n)
    def _(d):
        share_copy(d).start()

    out_ref[...] = partial[me]

    @pl.loop(1, n)
    def _(d):
        share_copy(d).wait()
        out_ref[...] += shares[d]


def fused(source, coords, meta, blocks, n):
    vis = coords.shape[2]
    table = pltpu.VMEM((vis // 128, GROUP * PITCH, 128), jnp.float32)
    vmem = pl.BlockSpec(memory_space=pltpu.VMEM)
    rows = 2 * BL_DEV
    sems = pltpu.SemaphoreType.DMA((n,))
    return pl.pallas_call(
        functools.partial(fused_kernel, n),
        out_shape=jax.ShapeDtypeStruct((rows, vis), jnp.float32),
        in_specs=[pl.BlockSpec(memory_space=pltpu.SMEM)] + [vmem] * 6,
        out_specs=vmem,
        scratch_shapes=[
            pltpu.VMEM((3, GROUP, vis), jnp.float32),
            pltpu.VMEM((n, 3, GROUP, vis), jnp.int16),
            pltpu.VMEM((n, 3, GROUP, vis), jnp.int16),
            pltpu.VMEM((n, 1, META), jnp.int32),
            pltpu.SMEM((n, 1, META), jnp.int32),
            pltpu.VMEM((blocks.shape[0], 2 * SUB, 4 * SUB), jnp.bfloat16),
            table,
            table,
            table,
            table,
            pltpu.VMEM((GROUP, vis), jnp.float32),
            pltpu.VMEM((GROUP, vis), jnp.float32),
            pltpu.VMEM((GROUP, 2 * vis), jnp.float32),
            pltpu.VMEM((n, rows, vis), jnp.float32),
            pltpu.VMEM((n, rows, vis), jnp.float32),
            sems,
            sems,
            sems,
            sems,
            sems,
            sems,
            pltpu.SemaphoreType.DMA,
        ],
        compiler_params=pltpu.CompilerParams(
            collective_id=0, has_side_effects=True, vmem_limit_bytes=40 * 1024 * 1024
        ),
        cost_estimate=pl.CostEstimate(
            flops=n * GROUP * 128 * 128 * 768, bytes_accessed=4 * n * GROUP * 3 * vis, transcendentals=0
        ),
    )(source, coords, meta, blocks, *fold_matrices())


def body(model_blocks, task_owner, task_block, baseline_of_task, coords, vis_count):
    facets = lax.axis_size("fac")
    tasks, _, vis = coords.shape
    capacity = max(2, 2 * tasks // facets)
    slots = facets * capacity
    owner = task_owner[:, 0]
    same = owner[:, None] == owner[None, :]
    before = jnp.arange(tasks)[None, :] < jnp.arange(tasks)[:, None]
    rank = jnp.sum((same & before).astype(jnp.int32), axis=1)
    slot = owner * capacity + rank
    hit = jnp.arange(slots, dtype=jnp.int32)[:, None] == slot[None, :]
    source = jnp.sum(jnp.where(hit, jnp.arange(tasks, dtype=jnp.int32)[None, :], 0), axis=1)
    if capacity == GROUP:
        row = (baseline_of_task // BL_DEV) * (2 * BL_DEV) + baseline_of_task % BL_DEV
        none = jnp.zeros_like(row)
        meta = jnp.stack([vis_count, task_block, none, none, row, row + BL_DEV, row, row + BL_DEV])
        meta = jnp.where(hit.reshape(facets, 1, capacity, tasks), meta[None, :, None, :], 0)
        meta = jnp.sum(meta, axis=3).reshape(facets, 1, META)
        blocks = model_blocks.reshape(model_blocks.shape[0], 2 * SUB, 2 * SUB)
        share = fused(source, coords.transpose(1, 0, 2), meta, blocks, facets)
        return share.reshape(2, BL_DEV, vis).transpose(1, 0, 2)
    meta = jnp.stack([vis_count, task_block, baseline_of_task], axis=1)
    meta = jnp.sum(jnp.where(hit[:, :, None], meta[None], 0), axis=1)
    meta = jnp.pad(meta, ((0, 0), (0, META - 3)))
    meta = meta.astype(jnp.float32)
    rows = coords.reshape(tasks, 3 * vis)[source]
    sent = jnp.concatenate([rows, meta], axis=1)
    sent = sent.reshape(facets, capacity, 3 * vis + META)
    got = lax.all_to_all(sent, "fac", split_axis=0, concat_axis=0, tiled=True).reshape(slots, 3 * vis + META)
    folded = fold_blocks(model_blocks)
    block_ids = got[:, 3 * vis + 1].astype(jnp.int32)
    baselines = got[:, 3 * vis + 2].astype(jnp.int32)
    partial = compute(got, block_ids, baselines, folded, BL_DEV * facets, vis)
    shares = partial.reshape(facets, BL_DEV, 2 * vis)
    shares = lax.all_to_all(shares, "fac", split_axis=0, concat_axis=0, tiled=True)
    return jnp.sum(shares, axis=0).reshape(BL_DEV, 2, vis)


def solution(mesh):
    placed = (
        P(("grp", "fac"), None),
        P(("grp", "fac"), None),
        P(("grp", "fac")),
        P(("grp", "fac")),
        P(("grp", "fac"), None, None),
        P(("grp", "fac")),
    )
    return jax.shard_map(
        body, mesh=mesh, in_specs=placed, out_specs=P(("grp", "fac"), None, None), check_vma=False
    )
```

```python
import functools
import math

import jax
import jax.numpy as jnp
import numpy as np
from jax import lax
from jax.experimental import pallas as pl
from jax.experimental.pallas import tpu as pltpu
from jax.sharding import PartitionSpec as P

SUB = 64
HALF = SUB // 2
LAYERS = 2
BL_DEV = 4
GROUP = 16
META = 128
PITCH = 33
STEPS = 16383.5
MESH = pl.DeviceIdType.MESH


def fold_blocks(model_blocks):
    blocks = model_blocks.shape[0]
    pixels = model_blocks.reshape(blocks * LAYERS * 2 * SUB, SUB)
    fold = np.zeros((SUB, SUB), np.float32)
    for n in range(HALF):
        fold[HALF + n, n] = fold[HALF - 1 - n, n] = 1.0
        fold[HALF + n, HALF + n], fold[HALF - 1 - n, HALF + n] = 1.0, -1.0
    fold = jnp.asarray(fold, jnp.bfloat16)
    x = jnp.dot(pixels, fold, preferred_element_type=jnp.float32)
    x = x.reshape(blocks, LAYERS, 2, SUB, SUB)
    plus, minus = x[:, 0] + x[:, 1], x[:, 0] - x[:, 1]
    x = jnp.stack([plus, minus], axis=1)
    upper, lower = x[:, :, :, HALF:], x[:, :, :, HALF - 1 :: -1]
    even, odd = upper + lower, upper - lower

    def parts(rows, turn):
        out_re, out_im = [], []
        for k in range(2):
            for m in range(2):
                re = rows[:, k, 0, :, m * HALF : (m + 1) * HALF]
                im = rows[:, k, 1, :, m * HALF : (m + 1) * HALF]
                times = (k - m + turn) % 4
                for _ in range(times):
                    re, im = -im, re
                out_re.append(re)
                out_im.append(im)
        return jnp.concatenate(out_re, axis=2), jnp.concatenate(out_im, axis=2)

    even_re, even_im = parts(even, 0)
    odd_re, odd_im = parts(odd, 3)
    return jnp.concatenate([even_re, even_im, odd_re, odd_im], axis=1).astype(jnp.bfloat16)


def sincos(x):
    n = jnp.floor(x + 0.5)
    t = (x - n) * (0.5 * math.pi)
    t2 = t * t
    s = t * (1.0 + t2 * (-1.0 / 6 + t2 * (1.0 / 120 + t2 * (-1.0 / 5040 + t2 * (1.0 / 362880)))))
    c = 1.0 + t2 * (-0.5 + t2 * (1.0 / 24 + t2 * (-1.0 / 720 + t2 * (1.0 / 40320 - t2 * (1.0 / 3628800)))))
    turn = n.astype(jnp.int32)
    swap = (turn & 1) == 1
    sine = jnp.where(swap, c, s)
    cosine = jnp.where(swap, s, c)
    sine = jnp.where((turn & 2) == 2, -sine, sine)
    cosine = jnp.where(((turn + 1) & 2) == 2, -cosine, cosine)
    return sine, cosine


def powers(x, cos_ref, sin_ref):
    s0, c0 = sincos(0.5 * x)
    twice = 2.0 - 4.0 * s0 * s0
    s, c, s_last, c_last = s0, c0, -s0, c0
    lanes = x.shape[1] // 128
    for p in range(HALF):
        for a in range(lanes):
            cos_ref[a, pl.ds(p, GROUP, stride=PITCH), :] = c[:, a * 128 : (a + 1) * 128]
            sin_ref[a, pl.ds(p, GROUP, stride=PITCH), :] = s[:, a * 128 : (a + 1) * 128]
        if p < HALF - 1:
            s, c, s_last, c_last = twice * s - s_last, twice * c - c_last, s, c
    return s0, c0


def load(ref, t):
    lanes = ref.shape[0]
    return jnp.concatenate([ref[a, pl.ds(t * PITCH, HALF), :] for a in range(lanes)], axis=1)


def compute_kernel(block_ids, baselines, slots_ref, folded_ref, out_ref, ru, su, rv, sv, cw_ref, sw_ref, sums):
    g = pl.program_id(0)
    vis = out_ref.shape[1] // 2

    @pl.when(g == 0)
    def _():
        out_ref[...] = jnp.zeros_like(out_ref)

    u, v, w = (slots_ref[:, i * vis : (i + 1) * vis] for i in range(3))
    us, uc = powers(u, ru, su)
    vs, vc = powers(v, rv, sv)
    ws, wc = sincos(2.0 * w)
    cw_ref[...] = wc
    sw_ref[...] = ws
    for t in range(GROUP):
        c, s = load(rv, t), load(sv, t)
        cw, sw = cw_ref[t : t + 1, :], sw_ref[t : t + 1, :]
        basis = jnp.concatenate([c * cw, s * cw, c * sw, s * sw], axis=0).astype(jnp.bfloat16)
        inner = jnp.dot(folded_ref[block_ids[g * GROUP + t]], basis, preferred_element_type=jnp.float32)
        rc, rs = load(ru, t), load(su, t)
        re = jnp.sum(rc * inner[:HALF] + rs * inner[2 * HALF : 3 * HALF], axis=0, keepdims=True)
        im = jnp.sum(rc * inner[HALF : 2 * HALF] + rs * inner[3 * HALF :], axis=0, keepdims=True)
        sums[t : t + 1, :vis] = re
        sums[t : t + 1, vis:] = im
    hc, hs = uc * vc - us * vs, uc * vs + us * vc
    re, im = sums[:, :vis], sums[:, vis:]
    live = lax.broadcasted_iota(jnp.int32, (GROUP, vis), 1).astype(jnp.float32) < slots_ref[:, 3 * vis : 3 * vis + 1]
    sums[:, :vis] = jnp.where(live, re * hc - im * hs, 0.0)
    sums[:, vis:] = jnp.where(live, re * hs + im * hc, 0.0)
    for t in range(GROUP):
        b = baselines[g * GROUP + t]
        out_ref[pl.ds(b, 1), :] += sums[t : t + 1, :]


def compute(slots, block_ids, baselines, folded, n_baselines, vis):
    n, width = slots.shape
    lanes = vis // 128
    table = pltpu.VMEM((lanes, (GROUP + 1) * PITCH, 128), jnp.float32)
    return pl.pallas_call(
        compute_kernel,
        out_shape=jax.ShapeDtypeStruct((n_baselines, 2 * vis), jnp.float32),
        grid_spec=pltpu.PrefetchScalarGridSpec(
            num_scalar_prefetch=2,
            grid=(n // GROUP,),
            in_specs=[
                pl.BlockSpec((GROUP, width), lambda g, *_: (g, 0)),
                pl.BlockSpec(folded.shape, lambda g, *_: (0, 0, 0)),
            ],
            out_specs=pl.BlockSpec((n_baselines, 2 * vis), lambda g, *_: (0, 0)),
            scratch_shapes=[
                table,
                table,
                table,
                table,
                pltpu.VMEM((GROUP, vis), jnp.float32),
                pltpu.VMEM((GROUP, vis), jnp.float32),
                pltpu.VMEM((GROUP, 2 * vis), jnp.float32),
            ],
        ),
        compiler_params=pltpu.CompilerParams(vmem_limit_bytes=32 * 1024 * 1024),
        cost_estimate=pl.CostEstimate(flops=n * 128 * 128 * 768, bytes_accessed=4 * n * width, transcendentals=0),
    )(block_ids, baselines, slots, folded)


def fold_matrices():
    one = np.zeros((SUB, SUB), np.float32)
    for n in range(HALF):
        one[HALF + n, n] = one[HALF - 1 - n, n] = 1.0
        one[HALF + n, HALF + n], one[HALF - 1 - n, HALF + n] = 1.0, -1.0
    by_layer = []
    for sign in (1.0, -1.0):
        pair = np.concatenate([one, sign * one], axis=1)
        zero = np.zeros_like(pair)
        by_layer.append(np.block([[pair, zero], [zero, pair]]))
    rows = one.T.reshape(SUB, HALF, 2).transpose(0, 2, 1).reshape(SUB, SUB)
    rows = np.concatenate([rows, rows], axis=1)
    return tuple(jnp.asarray(x, jnp.bfloat16) for x in (*by_layer, rows))


def fold_one(pixels, right0, right1, left):
    y = jnp.dot(pixels[:SUB], right0, preferred_element_type=jnp.float32)
    y = y + jnp.dot(pixels[SUB:], right1, preferred_element_type=jnp.float32)
    wide = 2 * SUB
    z = []
    for c in range(2):
        part = y[c * HALF : (c + 1) * HALF]
        part = jnp.concatenate([part[:, :wide], part[:, wide:]], axis=0)
        high = part.astype(jnp.bfloat16)
        low = (part - high.astype(jnp.float32)).astype(jnp.bfloat16)
        z.append(jnp.dot(left, jnp.concatenate([high, low], axis=0), preferred_element_type=jnp.float32))
    re, im = z
    term = lax.broadcasted_iota(jnp.int32, (HALF, wide), 1) // HALF

    def pick(a, b, c, d):
        return jnp.where(term == 0, a, jnp.where(term == 1, b, jnp.where(term == 2, c, d)))

    ere, eim, ore, oim = re[:HALF], im[:HALF], re[HALF:], im[HALF:]
    rows = [
        pick(ere, eim, -eim, ere),
        pick(eim, -ere, ere, eim),
        pick(oim, -ore, ore, oim),
        pick(-ore, -oim, oim, -ore),
    ]
    rows = jnp.concatenate(rows, axis=0)
    high = rows.astype(jnp.bfloat16)
    return jnp.concatenate([high, (rows - high.astype(jnp.float32)).astype(jnp.bfloat16)], axis=1)


def fused_kernel(
    n, source, coords_ref, meta_ref, blocks_ref, right0, right1, left, out_ref,
    stage, send, recv, meta_recv, meta_smem, folded, ru, su, rv, sv, cw_ref, sw_ref, sums, partial, shares,
    send_sem, recv_sem, meta_send, meta_got, share_send, share_got, local_sem,
):
    vis = coords_ref.shape[2]
    meta_lane = lax.broadcasted_iota(jnp.int32, (GROUP, META), 1)
    meta_row = lax.broadcasted_iota(jnp.int32, (GROUP, META), 0)
    me = lax.axis_index("fac")
    barrier = pltpu.get_barrier_semaphore()

    def peer_of(d):
        return lax.rem(me + d, n)

    @pl.loop(1, n)
    def _(d):
        pl.semaphore_signal(barrier, inc=1, device_id={"fac": peer_of(d)}, device_id_type=MESH)

    def pack(d, to):
        peer = peer_of(d)
        for r in range(GROUP):
            task = source[peer * GROUP + r]
            for i in range(3):
                stage[i, r : r + 1, :] = coords_ref[i, pl.ds(task, 1), :]
        to[d] = jnp.floor(stage[...] * STEPS + 0.5).astype(jnp.int32).astype(jnp.int16)

    pack(0, recv)
    meta_recv[0] = meta_ref[me]
    partial[...] = jnp.zeros_like(partial)

    @pl.loop(0, blocks_ref.shape[0], step=8)
    def _(b):
        for i in range(8):
            folded[b + i] = fold_one(blocks_ref[b + i], right0[...], right1[...], left[...])


    def meta_copy(d):
        return pltpu.make_async_remote_copy(
            src_ref=meta_ref.at[peer_of(d)], dst_ref=meta_recv.at[d], send_sem=meta_send.at[d],
            recv_sem=meta_got.at[d], device_id={"fac": peer_of(d)}, device_id_type=MESH,
        )

    def slot_copy(d):
        return pltpu.make_async_remote_copy(
            src_ref=send.at[d], dst_ref=recv.at[d], send_sem=send_sem.at[d],
            recv_sem=recv_sem.at[d], device_id={"fac": peer_of(d)}, device_id_type=MESH,
        )

    pl.semaphore_wait(barrier, n - 1)

    @pl.loop(1, n)
    def _(d):
        meta_copy(d).start()

    @pl.loop(1, n)
    def _(d):
        pack(d, send)
        slot_copy(d).start()

    @pl.loop(1, n)
    def _(d):
        meta_copy(d).wait()

    to_scalars = pltpu.make_async_copy(meta_recv, meta_smem, local_sem)
    to_scalars.start()
    to_scalars.wait()

    @pl.loop(0, n)
    def _(d):
        @pl.when(d > 0)
        def _():
            slot_copy(d).wait()

        u, v, w = (recv[d, i].astype(jnp.int32).astype(jnp.float32) * (1.0 / STEPS) for i in range(3))
        us, uc = powers(u, ru, su)
        vs, vc = powers(v, rv, sv)
        ws, wc = sincos(2.0 * w)
        cw_ref[...] = wc
        sw_ref[...] = ws
        for t in range(GROUP):
            c, s = load(rv, t), load(sv, t)
            cw, sw = cw_ref[t : t + 1, :], sw_ref[t : t + 1, :]
            basis = jnp.concatenate([c * cw, s * cw, c * sw, s * sw], axis=0).astype(jnp.bfloat16)
            basis = jnp.concatenate([basis, basis], axis=0)
            inner = jnp.dot(folded[meta_smem[d, 0, GROUP + t]], basis, preferred_element_type=jnp.float32)
            rc, rs = load(ru, t), load(su, t)
            re = jnp.sum(rc * inner[:HALF] + rs * inner[2 * HALF : 3 * HALF], axis=0, keepdims=True)
            im = jnp.sum(rc * inner[HALF : 2 * HALF] + rs * inner[3 * HALF :], axis=0, keepdims=True)
            sums[t : t + 1, :vis] = re
            sums[t : t + 1, vis:] = im
        hc, hs = uc * vc - us * vs, uc * vs + us * vc
        re, im = sums[:, :vis], sums[:, vis:]
        meta = meta_recv[d]
        count = jnp.sum(jnp.where(meta_lane == meta_row, meta.astype(jnp.float32), 0.0), axis=1, keepdims=True)
        live = lax.broadcasted_iota(jnp.int32, (GROUP, vis), 1).astype(jnp.float32) < count
        both = jnp.concatenate([re * hc - im * hs, re * hs + im * hc], axis=0)
        both = jnp.where(jnp.concatenate([live, live], axis=0), both, 0.0)
        high = both.astype(jnp.bfloat16).astype(jnp.float32)
        both = jnp.concatenate([high, both - high], axis=0).astype(jnp.bfloat16)
        onehot = lax.broadcasted_iota(jnp.int32, (n * 2 * BL_DEV, 4 * GROUP), 0) == meta[:, 4 * GROUP :]
        onehot = jnp.where(onehot, 1.0, 0.0).astype(jnp.bfloat16)
        added = jnp.dot(onehot, both, preferred_element_type=jnp.float32)
        partial[...] += added.reshape(partial.shape)

    def share_copy(d):
        return pltpu.make_async_remote_copy(
            src_ref=partial.at[peer_of(d)], dst_ref=shares.at[d], send_sem=share_send.at[d],
            recv_sem=share_got.at[d], device_id={"fac": peer_of(d)}, device_id_type=MESH,
        )

    @pl.loop(1, n)
    def _(d):
        share_copy(d).start()

    out_ref[...] = partial[me]

    @pl.loop(1, n)
    def _(d):
        share_copy(d).wait()
        out_ref[...] += shares[d]


def fused(source, coords, meta, blocks, n):
    vis = coords.shape[2]
    table = pltpu.VMEM((vis // 128, (GROUP + 1) * PITCH, 128), jnp.float32)
    vmem = pl.BlockSpec(memory_space=pltpu.VMEM)
    rows = 2 * BL_DEV
    sems = pltpu.SemaphoreType.DMA((n,))
    return pl.pallas_call(
        functools.partial(fused_kernel, n),
        out_shape=jax.ShapeDtypeStruct((rows, vis), jnp.float32),
        in_specs=[pl.BlockSpec(memory_space=pltpu.SMEM)] + [vmem] * 6,
        out_specs=vmem,
        scratch_shapes=[
            pltpu.VMEM((3, GROUP, vis), jnp.float32),
            pltpu.VMEM((n, 3, GROUP, vis), jnp.int16),
            pltpu.VMEM((n, 3, GROUP, vis), jnp.int16),
            pltpu.VMEM((n, 1, META), jnp.int32),
            pltpu.SMEM((n, 1, META), jnp.int32),
            pltpu.VMEM((blocks.shape[0], 2 * SUB, 4 * SUB), jnp.bfloat16),
            table,
            table,
            table,
            table,
            pltpu.VMEM((GROUP, vis), jnp.float32),
            pltpu.VMEM((GROUP, vis), jnp.float32),
            pltpu.VMEM((GROUP, 2 * vis), jnp.float32),
            pltpu.VMEM((n, rows, vis), jnp.float32),
            pltpu.VMEM((n, rows, vis), jnp.float32),
            sems,
            sems,
            sems,
            sems,
            sems,
            sems,
            pltpu.SemaphoreType.DMA,
        ],
        compiler_params=pltpu.CompilerParams(
            collective_id=0, has_side_effects=True, vmem_limit_bytes=40 * 1024 * 1024
        ),
        cost_estimate=pl.CostEstimate(
            flops=n * GROUP * 128 * 128 * 768, bytes_accessed=4 * n * GROUP * 3 * vis, transcendentals=0
        ),
    )(source, coords, meta, blocks, *fold_matrices())


def body(model_blocks, task_owner, task_block, baseline_of_task, coords, vis_count):
    facets = lax.axis_size("fac")
    tasks, _, vis = coords.shape
    capacity = max(2, 2 * tasks // facets)
    slots = facets * capacity
    owner = task_owner[:, 0]
    same = owner[:, None] == owner[None, :]
    before = jnp.arange(tasks)[None, :] < jnp.arange(tasks)[:, None]
    rank = jnp.sum((same & before).astype(jnp.int32), axis=1)
    slot = owner * capacity + rank
    hit = jnp.arange(slots, dtype=jnp.int32)[:, None] == slot[None, :]
    source = jnp.sum(jnp.where(hit, jnp.arange(tasks, dtype=jnp.int32)[None, :], 0), axis=1)
    if capacity == GROUP:
        row = (baseline_of_task // BL_DEV) * (2 * BL_DEV) + baseline_of_task % BL_DEV
        none = jnp.zeros_like(row)
        meta = jnp.stack([vis_count, task_block, none, none, row, row + BL_DEV, row, row + BL_DEV])
        meta = jnp.where(hit.reshape(facets, 1, capacity, tasks), meta[None, :, None, :], 0)
        meta = jnp.sum(meta, axis=3).reshape(facets, 1, META)
        blocks = model_blocks.reshape(model_blocks.shape[0], 2 * SUB, 2 * SUB)
        share = fused(source, coords.transpose(1, 0, 2), meta, blocks, facets)
        return share.reshape(2, BL_DEV, vis).transpose(1, 0, 2)
    meta = jnp.stack([vis_count, task_block, baseline_of_task], axis=1)
    meta = jnp.sum(jnp.where(hit[:, :, None], meta[None], 0), axis=1)
    meta = jnp.pad(meta, ((0, 0), (0, META - 3)))
    meta = meta.astype(jnp.float32)
    rows = coords.reshape(tasks, 3 * vis)[source]
    sent = jnp.concatenate([rows, meta], axis=1)
    sent = sent.reshape(facets, capacity, 3 * vis + META)
    got = lax.all_to_all(sent, "fac", split_axis=0, concat_axis=0, tiled=True).reshape(slots, 3 * vis + META)
    folded = fold_blocks(model_blocks)
    block_ids = got[:, 3 * vis + 1].astype(jnp.int32)
    baselines = got[:, 3 * vis + 2].astype(jnp.int32)
    partial = compute(got, block_ids, baselines, folded, BL_DEV * facets, vis)
    shares = partial.reshape(facets, BL_DEV, 2 * vis)
    shares = lax.all_to_all(shares, "fac", split_axis=0, concat_axis=0, tiled=True)
    return jnp.sum(shares, axis=0).reshape(BL_DEV, 2, vis)


def solution(mesh):
    placed = (
        P(("grp", "fac"), None),
        P(("grp", "fac"), None),
        P(("grp", "fac")),
        P(("grp", "fac")),
        P(("grp", "fac"), None, None),
        P(("grp", "fac")),
    )
    return jax.shard_map(
        body, mesh=mesh, in_specs=placed, out_specs=P(("grp", "fac"), None, None), check_vma=False
    )
```
